32 devices in a mesh: dp: 2 (over core), cent: 16 (over z, y, x).
Axes of the slice: x: 2, y: 2, z: 4, core: 2. Of those that a mesh axis runs over, the one named last changes fastest.
Arguments:
- embeddings: bfloat16 [16384, 1024], P(('dp', 'cent')), may hold values from -44.5 to 53.875
- centroids: float32 [8192, 1024], P(('dp', 'cent')), may hold values from -3 to 5
- candidates: int32 [64, 8], P(('dp', 'cent')), may hold values from 0 to 15, all different within a row; in each aligned block of 32 rows (0 to 31, 32 to 63, ...) at most 24 rows name the same one
Outputs:
- new_centroids: float32 [8192, 1024], P(('dp', 'cent'))
- log_norm: float32 [16384], P(('dp', 'cent'))
- objective: float32 [], replicated
The draws below stay inside these ranges and needn't reach their ends.
Inputs may be any that keep to these rules, and one draw needn't show every extreme that they name: `candidates`: the 8 entries of a row block are different. Among the row blocks of one coarse group (aligned runs of 32 row blocks), no centroid block is named more than 24 times, and some centroid block is named exactly 24 times in every draw.
All inputs are finite; a program needn't handle non-finite values.
Results may differ from the reference program's by a relative error of at most 0.0067.
Values may be sent and summed in bfloat16 or wider, within the bound.
A program may use at most 128 MiB of HBM per device.

```python
import math
import jax
import jax.numpy as jnp
import numpy as np
from jax import lax

D = 1024
BLK = 256
TOPC = 8
CB_DEV = 1
RB_DEV = 2
GROUP_BLOCKS = 16
MOST = 24
K = 8192
NRB = 64
NROWS = 16384
N_DP = 2
N_CENT = 16


def centroid_noise(key):
    noise_key = jax.random.fold_in(key, 21)
    noise = jnp.clip(jax.random.normal(noise_key, (K, D), jnp.float32), -4.0, 4.0)
    return noise


def draw_centroids(key, part):
    return 1.0 + centroid_noise(key)


def draw_embeddings(key, part):
    noise_key = jax.random.fold_in(key, 11)
    pick_key = jax.random.fold_in(key, 12)
    level_key = jax.random.fold_in(key, 13)
    jitter_key = jax.random.fold_in(key, 14)
    partner_key = jax.random.fold_in(key, 15)
    strength_key = jax.random.fold_in(key, 16)
    noise = jnp.clip(jax.random.normal(noise_key, (NROWS, D), jnp.float32), -6.0, 6.0)
    group_size = RB_DEV * BLK * (GROUP_BLOCKS // CB_DEV)
    group_count = NROWS // group_size
    group_cents = GROUP_BLOCKS * BLK
    row_index = jnp.arange(NROWS, dtype=jnp.int32)
    group_of_row = row_index // group_size
    jitter = jax.random.randint(jitter_key, (group_count,), 0, 160)
    trend = 160 * jnp.arange(group_count, dtype=jnp.int32) // max(group_count - 1, 1)
    threshold = jitter + trend
    lifted = jax.random.randint(pick_key, (NROWS,), 0, 4096) < threshold[group_of_row]
    lifted = jnp.logical_or(lifted, row_index == 0)
    level = jax.random.uniform(level_key, (NROWS,), jnp.float32, 120.0, 320.0)
    offset = jnp.where(lifted, 0.5 + level / math.sqrt(D), 0.0)
    partner = group_of_row * group_cents + jax.random.randint(partner_key, (NROWS,), 0, group_cents)
    strength = jax.random.uniform(strength_key, (NROWS,), jnp.float32, 128.0, 288.0) / math.sqrt(D)
    strength = jnp.where(lifted, strength, 0.0)
    aligned = centroid_noise(key)[partner]
    return (noise + offset[:, None] + strength[:, None] * aligned).astype(jnp.bfloat16)


def shared_out(rng, own, number, rows, amount, top, most, slope):
    sequence = jax.random.permutation(rng, amount)
    crowded, common = load_shares(amount, rows * top, most, slope, True), load_shares(amount, rows * top, most, slope, False)
    places = jnp.arange(amount)

    def named(tallies, rotation):
        used = int((tallies > 0).sum())
        fixed = max(1, used // 4)
        moved = fixed + (places - fixed + rotation * (used - fixed)) % max(1, amount - fixed)
        return jnp.zeros((amount,), jnp.int32).at[sequence[jnp.where(places < fixed, places, moved)]].set(jnp.asarray(tallies, jnp.int32))

    tallies = jnp.where(number % 4 == 0, named(crowded, number // 4), named(common, number - number // 4 - 1))
    mixed = jax.random.permutation(jax.random.fold_in(own, 3), amount)
    donor, receiver = mixed[0:amount // 2 * 2:2], mixed[1:amount // 2 * 2:2]
    margin = jnp.minimum(tallies[donor] - 1, most - tallies[receiver]) // 2
    margin = jnp.where((donor == sequence[0]) | (receiver == sequence[0]) | (tallies[receiver] == 0), 0, jnp.maximum(margin, 0))
    moved = jax.random.randint(jax.random.fold_in(own, 4), (amount // 2,), 0, 1 << 20) % (margin + 1)
    tallies = tallies.at[donor].add(-moved).at[receiver].add(moved)
    items = jnp.searchsorted(jnp.cumsum(tallies), jnp.arange(rows * top), side="right").astype(jnp.int32)
    grid = items.reshape(top, rows).T
    grid = grid[jax.random.permutation(jax.random.fold_in(own, 1), rows)]
    rotation = jax.random.randint(jax.random.fold_in(own, 2), (rows, 1), 0, top)
    return jnp.take_along_axis(grid, (jnp.arange(top)[None, :] + rotation) % top, axis=1)


def load_shares(number_of, total, most, lean, full):
    portions = [(1 << 20) // math.isqrt(grade ** lean) + 1 for grade in range(1, number_of + 1)]
    largest = most if full else min(most, max(-(-total // number_of), total * portions[0] // sum(portions)))
    least = 1 if total - largest >= number_of - 1 else 0
    holding, spare = [largest] + [least] * (number_of - 1), total - largest - least * (number_of - 1)
    while spare > 0:
        free = [i for i in range(1, number_of) if holding[i] < largest] or [i for i in range(1, number_of) if holding[i] < most]
        whole, budget = sum([portions[i] for i in free]), spare
        for i in free:
            more = min(most - holding[i], max(1, budget * portions[i] // whole), spare)
            holding[i] = holding[i] + more
            spare = spare - more
    return np.array(holding)


def setup_inputs(seed: int = 0) -> dict:
    key_of = jax.random.split(jax.random.key(seed), 4)
    embeddings = draw_embeddings(jax.random.fold_in(key_of[3], 71), 0)
    centroids = draw_centroids(jax.random.fold_in(key_of[3], 71), 0)
    candidates_keys = jax.random.split(jax.random.fold_in(key_of[2], 1), NRB // (RB_DEV * N_CENT))
    candidates_turns = jax.random.permutation(jax.random.fold_in(key_of[2], 3), NRB // (RB_DEV * N_CENT))
    candidates = jax.vmap(lambda own, number: shared_out(jax.random.fold_in(key_of[2], 2), own, number, RB_DEV * N_CENT, CB_DEV * N_CENT, TOPC, MOST, 2))(candidates_keys, candidates_turns).reshape((NRB, TOPC))
    return {"embeddings": embeddings, "centroids": centroids, "candidates": candidates}


def group_update(group_rows, group_cents, group_lists):
    cent_bf = lax.optimization_barrier(group_cents.astype(jnp.bfloat16))
    half_norm = 0.5 * lax.optimization_barrier(jnp.sum(group_cents * group_cents, axis=2))

    def row_step(carry, inputs):
        block_sums, block_counts = carry
        row_block, id_list = inputs
        chosen = cent_bf[id_list].astype(jnp.float32)
        row_values = row_block.astype(jnp.float32)
        dot_scores = jnp.einsum('bd,tkd->btk', row_values, chosen, precision=lax.Precision.HIGHEST)
        logits = (dot_scores - half_norm[id_list][None]) / math.sqrt(D)
        peak_value = lax.optimization_barrier(jnp.max(logits, axis=(1, 2)))
        row_log = peak_value + jnp.log(lax.optimization_barrier(jnp.sum(jnp.exp(logits - peak_value[:, None, None]), axis=(1, 2))))
        weights = jnp.exp(logits - row_log[:, None, None])
        block_counts = block_counts.at[id_list].add(lax.optimization_barrier(jnp.sum(weights, axis=0)))
        weights_bf = lax.optimization_barrier(weights.astype(jnp.bfloat16)).astype(jnp.float32)
        block_terms = jnp.einsum('btk,bd->tkd', weights_bf, row_values, precision=lax.Precision.HIGHEST)
        block_sums = block_sums.at[id_list].add(block_terms)
        return ((block_sums, block_counts), row_log)
    zero_sums = jnp.zeros(group_cents.shape, jnp.float32)
    zero_counts = jnp.zeros(group_cents.shape[:2], jnp.float32)
    (block_sums, block_counts), row_logs = lax.scan(row_step, (zero_sums, zero_counts), (group_rows, group_lists))
    new_cents = (block_sums + group_cents) / (block_counts[..., None] + 1.0)
    return (new_cents, row_logs)

def group_apply(inputs):
    return group_update(inputs[0], inputs[1], inputs[2])

def reference(embeddings, centroids, candidates):
    row_groups = embeddings.reshape(N_DP, RB_DEV * N_CENT, BLK, D)
    cent_groups = centroids.reshape(N_DP, GROUP_BLOCKS, BLK, D)
    list_groups = candidates.reshape(N_DP, RB_DEV * N_CENT, TOPC)
    new_cents, row_logs = lax.map(group_apply, (row_groups, cent_groups, list_groups))
    log_norm = row_logs.reshape(NROWS)
    objective = jnp.sum(log_norm) / NROWS
    return (new_cents.reshape(K, D), log_norm, objective)
```

```python
import functools
import math

import jax
import jax.numpy as jnp
from jax import lax
from jax.experimental import pallas as pl
from jax.experimental.pallas import tpu as pltpu
from jax.sharding import PartitionSpec as P

BLK = 256
PLANE = 4
FLOOR = -1e30
MESH = pl.DeviceIdType.MESH


def kernel(
    nd, nz, row_total,
    emb_ref, cent_ref, mask_ref,
    new_ref, log_ref, obj_ref,
    rbuf, cbuf, hnrow, hncol, maskbuf, pbuf, mst, sst, stat, fbuf, wbuf, part, tx, up_rx, dn_rx,
    cacc, cnt, cnt_rx, zsum, gsum,
    local_sem, row_s, row_r, mask_s, mask_r, hn_s, hn_r, cu_s, cu_r, cd_s, cd_r,
    st_s, st_r, zs_s, zs_r, gs_s, gs_r, ct_s, ct_r, up_s, up_r, dn_s, dn_r,
):
    d = lax.axis_index("dp")
    me = lax.axis_index("cent")
    p, q = me // PLANE, me % PLANE
    x, y = q % 2, q // 2
    qx, qy, qd = q + 1 - 2 * x, q + 2 - 4 * y, 3 - q
    last = nz - 1
    blk, dim = cent_ref.shape

    def at_plane(o):
        return {"cent": p * PLANE + o}

    def at_z(z):
        return {"cent": z * PLANE + q}

    def rows_at(o, b):
        return rbuf.at[pl.ds(pl.multiple_of((o * 2 + b) * BLK, BLK), BLK)]

    def remote(src, dst, s, r, to):
        return pltpu.make_async_remote_copy(
            src_ref=src, dst_ref=dst, send_sem=s, recv_sem=r, device_id=to, device_id_type=MESH
        )

    own_rows = pl.ds(pl.multiple_of(q * 2 * BLK, 2 * BLK), 2 * BLK)
    fetch = pltpu.make_async_copy(emb_ref, rbuf.at[own_rows], local_sem)
    fetch.start()

    barrier = pltpu.get_barrier_semaphore()
    for o in (qx, qy, qd):
        pl.semaphore_signal(barrier, inc=1, device_id=at_plane(o), device_id_type=MESH)
    for k in range(1, nz):
        pl.semaphore_signal(barrier, inc=1, device_id=at_z((p + k) % nz), device_id_type=MESH)
    for k in range(1, nd):
        pl.semaphore_signal(barrier, inc=1, device_id={"dp": (d + k) % nd}, device_id_type=MESH)

    cent = cent_ref[...]
    cbuf[p] = cent.astype(jnp.bfloat16)
    norm = 0.5 * jnp.sum(cent * cent, axis=1, keepdims=True)
    wide = jnp.broadcast_to(norm, (blk, 128))
    hncol[p] = wide
    hnrow[p] = wide.T[:8]
    maskbuf[pl.ds(q * 2, 2)] = mask_ref[...]
    fetch.wait()
    pl.semaphore_wait(barrier, 3 + (nz - 1) + (nd - 1))

    plane_peers = (qx, qy, qd)
    mine = maskbuf.at[pl.ds(q * 2, 2)]
    mask_out = [remote(mine, mine, mask_s.at[i], mask_r.at[i], at_plane(o)) for i, o in enumerate(plane_peers)]
    hn_out = [
        remote(hnrow.at[p], hnrow.at[p], hn_s.at[k - 1], hn_r.at[k - 1], at_z((p + k) % nz)) for k in range(1, nz)
    ]
    for c in mask_out + hn_out:
        c.start()

    def up_send(s):
        z = jnp.maximum(p - s, 0)
        return remote(cbuf.at[z], cbuf.at[z], cu_s.at[s], cu_r.at[s], at_z(jnp.minimum(p + 1, last)))

    def dn_send(s):
        z = jnp.minimum(p + s, last)
        return remote(cbuf.at[z], cbuf.at[z], cd_s.at[s], cd_r.at[s], at_z(jnp.maximum(p - 1, 0)))

    def up_wait(s):
        z = p - 1 - s
        remote(cbuf.at[z], cbuf.at[z], cu_s.at[s], cu_r.at[s], at_z(p - 1)).wait_recv()

    def dn_wait(s):
        z = p + 1 + s
        remote(cbuf.at[z], cbuf.at[z], cd_s.at[s], cd_r.at[s], at_z(p + 1)).wait_recv()

    def row_copy(i, o, b, to):
        return remote(rows_at(o, b), rows_at(o, b), row_s.at[i], row_r.at[i], at_plane(to))

    pl.when(p < last)(lambda: up_send(0).start())
    pl.when(p > 0)(lambda: dn_send(0).start())
    row_out = [
        row_copy(0, q, 0, qx),
        row_copy(1, q, 1, qy),
        row_copy(2, q, 1, qx),
        row_copy(3, q, 0, qy),
        row_copy(4, qx, 0, qy),
        row_copy(5, qy, 1, qx),
    ]
    for c in row_out[:4]:
        c.start()
    row_in = [
        row_copy(0, qx, 0, qx),
        row_copy(1, qy, 1, qy),
        row_copy(2, qx, 1, qx),
        row_copy(3, qy, 0, qy),
        row_copy(4, qd, 0, qy),
        row_copy(5, qd, 1, qx),
    ]

    for i, o in enumerate(plane_peers):
        there = maskbuf.at[pl.ds(o * 2, 2)]
        remote(there, there, mask_s.at[i], mask_r.at[i], at_plane(o)).wait_recv()
    for k in range(1, nz):
        z = (p + nz - k) % nz
        remote(hnrow.at[z], hnrow.at[z], hn_s.at[k - 1], hn_r.at[k - 1], at_z(z)).wait_recv()
        row = hnrow[z][:1]
        hncol[z] = jnp.broadcast_to(row, (128, blk)).T

    def pair(i, z):
        t, e = i // 2, i % 2
        mult = (t * (3 - t)) // 2
        late = mult * (t - 1)
        rel = t - late + mult * e
        b = e + late * (1 - 2 * e)
        rx, ry = rel % 2, rel // 2
        ox, oy = x + rx - 2 * x * rx, y + ry - 2 * y * ry
        ci = (oy * 2 + ox) * 2 + b
        start = pl.multiple_of(ci * BLK, BLK)
        dots = lax.dot_general(
            cbuf[z], rbuf[pl.ds(start, BLK), :], (((1,), (1,)), ((), ())), preferred_element_type=jnp.float32
        )
        bias = maskbuf[ci, pl.ds(z * PLANE + q, 1), :]
        bias = jnp.concatenate([bias] * (BLK // 128), axis=1)
        norm = jnp.concatenate([hncol[z]] * (BLK // 128), axis=1)
        logits = (dots - norm) * (1.0 / math.sqrt(dim)) + bias
        peak = jnp.max(logits, axis=0, keepdims=True)
        e_val = jnp.exp(logits - peak)
        pbuf[z, :, pl.ds(start, BLK)] = e_val
        mst[z, pl.ds(ci, 1), :] = peak
        sst[z, pl.ds(ci, 1), :] = jnp.sum(e_val, axis=0, keepdims=True)

    def pairs(row_lo, row_hi, z_lo, z_hi):
        count = row_hi - row_lo

        def body(n, carry):
            pair(row_lo + n % count, z_lo + n // count)
            return carry

        lax.fori_loop(0, count * (z_hi - z_lo), body, 0)

    pairs(0, 2, p, p + 1)
    for s in range(last):
        @pl.when(p - 1 - s >= 0)
        def _(s=s):
            up_wait(s)
            if s + 1 < last:
                pl.when(p < last)(lambda: up_send(s + 1).start())

        @pl.when(p + 1 + s <= last)
        def _(s=s):
            dn_wait(s)
            if s + 1 < last:
                pl.when(p > 0)(lambda: dn_send(s + 1).start())

        row_in[2 * s].wait_recv()
        row_in[2 * s + 1].wait_recv()
        if s == 0:
            row_out[4].start()
            row_out[5].start()
        have = 2 * s + 2

        @pl.when(p - 1 - s >= 0)
        def _(s=s, have=have):
            pairs(0, have, p - 1 - s, p - s)

        @pl.when(p + 1 + s <= last)
        def _(s=s, have=have):
            pairs(0, have, p + 1 + s, p + 2 + s)

        pairs(have, have + 2, jnp.maximum(p - s - 1, 0), jnp.minimum(p + s + 1, last) + 1)

    peak, total = mst[0], sst[0]
    for z in range(1, nz):
        peak = jnp.maximum(peak, mst[z])
    total = sum(sst[z] * jnp.exp(mst[z] - peak) for z in range(nz))
    stat[q, 0] = peak
    stat[q, 1] = total
    st_out = [
        remote(stat.at[q], stat.at[q], st_s.at[i], st_r.at[i], at_plane(o)) for i, o in enumerate(plane_peers)
    ]
    for c in st_out:
        c.start()
    for i, o in enumerate(plane_peers):
        remote(stat.at[o], stat.at[o], st_s.at[i], st_r.at[i], at_plane(o)).wait_recv()
    peak = stat[0, 0]
    for o in range(1, PLANE):
        peak = jnp.maximum(peak, stat[o, 0])
    total = sum(stat[o, 1] * jnp.exp(stat[o, 0] - peak) for o in range(PLANE))
    log_norm = peak + jnp.log(total)
    place = lax.broadcasted_iota(jnp.int32, log_norm.shape, 0)
    for r in range(2):
        log_ref[r : r + 1, :] = jnp.sum(jnp.where(place == q * 2 + r, log_norm, 0.0), axis=0, keepdims=True)
    for z in range(nz):
        fbuf[z] = jnp.exp(mst[z] - log_norm)
    zsum[p] = jnp.broadcast_to(jnp.sum(jnp.sum(log_norm, axis=1, keepdims=True), axis=0, keepdims=True), (8, 128))
    zs_out = [
        remote(zsum.at[p], zsum.at[p], zs_s.at[k - 1], zs_r.at[k - 1], at_z((p + k) % nz)) for k in range(1, nz)
    ]
    for c in zs_out:
        c.start()

    def partial(t):
        cacc[...] = jnp.zeros_like(cacc)

        def weigh(ci, carry):
            cols = pl.ds(pl.multiple_of(ci * BLK, BLK), BLK)
            w = pbuf[t, :, cols] * fbuf[t, pl.ds(ci, 1), :]
            wbuf[:, cols] = w.astype(jnp.bfloat16)
            acc = cacc[...]
            for j in range(BLK // 128):
                acc = acc + w[:, j * 128 : (j + 1) * 128]
            cacc[...] = acc
            return carry

        lax.fori_loop(0, 2 * PLANE, weigh, 0)
        col = jnp.broadcast_to(jnp.sum(cacc[...], axis=1, keepdims=True), (blk, 128))
        cnt[t] = col.T[:8]

        def tile(n, carry):
            cols = pl.ds(pl.multiple_of(n * BLK, BLK), BLK)
            part[t, :, cols] = jnp.dot(wbuf[...], rbuf[:, cols], preferred_element_type=jnp.float32)
            return carry

        lax.fori_loop(0, dim // BLK, tile, 0)

    def up_copy(t):
        return remote(tx.at[t], up_rx.at[t], up_s.at[t], up_r.at[t], at_z(jnp.minimum(p + 1, last)))

    def dn_copy(t):
        return remote(tx.at[t], dn_rx.at[t], dn_s.at[t], dn_r.at[t], at_z(jnp.maximum(p - 1, 0)))

    for s in range(last):
        up_t, dn_t = last - s, s

        @pl.when(p < up_t)
        def _(t=up_t):
            partial(t)

            @pl.when(p == 0)
            def _():
                tx[t] = part[t].astype(jnp.bfloat16)
                up_copy(t).start()

        @pl.when(p > dn_t)
        def _(t=dn_t):
            partial(t)

            @pl.when(p == last)
            def _():
                tx[t] = part[t].astype(jnp.bfloat16)
                dn_copy(t).start()

    partial(p)

    cnt_rx[p] = cnt[p]
    ct_out = [
        remote(cnt.at[(p + k) % nz], cnt_rx.at[p], ct_s.at[k - 1], ct_r.at[k - 1], at_z((p + k) % nz))
        for k in range(1, nz)
    ]
    for c in ct_out:
        c.start()

    for k in range(1, nz):
        z = (p + nz - k) % nz
        remote(zsum.at[z], zsum.at[z], zs_s.at[k - 1], zs_r.at[k - 1], at_z(z)).wait_recv()
    gsum[d] = sum(zsum[z] for z in range(nz))
    gs_out = [
        remote(gsum.at[d], gsum.at[d], gs_s.at[k - 1], gs_r.at[k - 1], {"dp": (d + k) % nd}) for k in range(1, nd)
    ]
    for c in gs_out:
        c.start()

    for s in range(last):
        up_t, dn_t = last - s, s

        @pl.when((p > 0) & (p < up_t))
        def _(t=up_t):
            up_copy(t).wait_recv()
            tx[t] = (part[t] + up_rx[t].astype(jnp.float32)).astype(jnp.bfloat16)
            up_copy(t).start()

        @pl.when((p < last) & (p > dn_t))
        def _(t=dn_t):
            dn_copy(t).wait_recv()
            tx[t] = (part[t] + dn_rx[t].astype(jnp.float32)).astype(jnp.bfloat16)
            dn_copy(t).start()

    for k in range(1, nz):
        z = (p + nz - k) % nz
        remote(cnt.at[z], cnt_rx.at[z], ct_s.at[k - 1], ct_r.at[k - 1], at_z(z)).wait_recv()
    counts = sum(cnt_rx[z] for z in range(nz))
    scale = 1.0 / (jnp.broadcast_to(counts[:1], (128, blk)).T[:, :1] + 1.0)
    for k in range(1, nd):
        o = (d + nd - k) % nd
        remote(gsum.at[o], gsum.at[o], gs_s.at[k - 1], gs_r.at[k - 1], {"dp": o}).wait_recv()
    obj_ref[...] = sum(gsum[o] for o in range(nd)) / row_total

    new_ref[...] = cent_ref[...] + part[p]

    @pl.when(p > 0)
    def _():
        up_copy(p).wait_recv()
        new_ref[...] += up_rx[p].astype(jnp.float32)

    @pl.when(p < last)
    def _():
        dn_copy(p).wait_recv()
        new_ref[...] += dn_rx[p].astype(jnp.float32)

    new_ref[...] = new_ref[...] * scale

    for c in mask_out + hn_out + row_out + st_out + zs_out + ct_out + gs_out:
        c.wait_send()
    for s in range(last):
        pl.when((p < last) & (p - s >= 0))(lambda s=s: up_send(s).wait_send())
        pl.when((p > 0) & (p + s <= last))(lambda s=s: dn_send(s).wait_send())
        pl.when(p < last - s)(lambda s=s: up_copy(last - s).wait_send())
        pl.when(p > s)(lambda s=s: dn_copy(s).wait_send())


def per_device(embeddings, centroids, candidates):
    nd, nc = lax.axis_size("dp"), lax.axis_size("cent")
    nz = nc // PLANE
    dim = embeddings.shape[1]
    rows = embeddings.shape[0]
    rb = candidates.shape[0]
    named = jnp.any(candidates[:, :, None] == jnp.arange(nc, dtype=jnp.int32), axis=1)
    mask = jnp.broadcast_to(jnp.where(named, 0.0, FLOOR).astype(jnp.float32)[:, :, None], (rb, nc, 128))
    f32, bf16 = jnp.float32, jnp.bfloat16
    nrb = rb * PLANE
    dma = pltpu.SemaphoreType.DMA
    vmem = pl.BlockSpec(memory_space=pltpu.VMEM)
    new, logs, obj = pl.pallas_call(
        functools.partial(kernel, nd, nz, float(rows * nd * nc)),
        out_shape=(
            jax.ShapeDtypeStruct((BLK, dim), f32),
            jax.ShapeDtypeStruct((rb, BLK), f32),
            jax.ShapeDtypeStruct((8, 128), f32),
        ),
        in_specs=[pl.BlockSpec(memory_space=pl.ANY), vmem, vmem],
        out_specs=(vmem, vmem, vmem),
        scratch_shapes=[
            pltpu.VMEM((nrb * BLK, dim), bf16),
            pltpu.VMEM((nz, BLK, dim), bf16),
            pltpu.VMEM((nz, 8, BLK), f32),
            pltpu.VMEM((nz, BLK, 128), f32),
            pltpu.VMEM((nrb, nc, 128), f32),
            pltpu.VMEM((nz, BLK, nrb * BLK), f32),
            pltpu.VMEM((nz, nrb, BLK), f32),
            pltpu.VMEM((nz, nrb, BLK), f32),
            pltpu.VMEM((PLANE, 2, nrb, BLK), f32),
            pltpu.VMEM((nz, nrb, BLK), f32),
            pltpu.VMEM((BLK, nrb * BLK), bf16),
            pltpu.VMEM((nz, BLK, dim), f32),
            pltpu.VMEM((nz, BLK, dim), bf16),
            pltpu.VMEM((nz, BLK, dim), bf16),
            pltpu.VMEM((nz, BLK, dim), bf16),
            pltpu.VMEM((BLK, 128), f32),
            pltpu.VMEM((nz, 8, BLK), f32),
            pltpu.VMEM((nz, 8, BLK), f32),
            pltpu.VMEM((nz, 8, 128), f32),
            pltpu.VMEM((nd, 8, 128), f32),
            dma(()),
            dma((6,)), dma((6,)),
            dma((3,)), dma((3,)),
            dma((nz - 1,)), dma((nz - 1,)),
            dma((nz - 1,)), dma((nz - 1,)),
            dma((nz - 1,)), dma((nz - 1,)),
            dma((3,)), dma((3,)),
            dma((nz - 1,)), dma((nz - 1,)),
            dma((max(nd - 1, 1),)), dma((max(nd - 1, 1),)),
            dma((nz - 1,)), dma((nz - 1,)),
            dma((nz,)), dma((nz,)),
            dma((nz,)), dma((nz,)),
        ],
        compiler_params=pltpu.CompilerParams(
            collective_id=0, has_side_effects=True, vmem_limit_bytes=48 * 1024 * 1024
        ),
    )(embeddings, centroids, mask)
    return new, logs.reshape(rows), obj[0, 0]


def solution(mesh):
    in_specs = (P(("dp", "cent"), None), P(("dp", "cent"), None), P(("dp", "cent"), None))
    out_specs = (P(("dp", "cent"), None), P(("dp", "cent")), P())
    return jax.shard_map(
        per_device, mesh=mesh, in_specs=in_specs, out_specs=out_specs, check_vma=False
    )
```

```python
import functools
import math

import jax
import jax.numpy as jnp
from jax import lax
from jax.experimental import pallas as pl
from jax.experimental.pallas import tpu as pltpu
from jax.sharding import PartitionSpec as P

BLK = 256
PLANE = 4
HALVES = 2
FLOOR = -1e30
MESH = pl.DeviceIdType.MESH


def kernel(
    nd, nz, row_total,
    emb_ref, cent_ref, mask_ref,
    new_ref, log_ref, obj_ref,
    rbuf, cbuf, hnrow, hncol, maskbuf, pbuf, mst, sst, stat, fbuf, wbuf, part, tx, up_rx, dn_rx,
    cacc, cnt, cnt_rx, zsum, gsum,
    local_sem, row_s, row_r, mask_s, mask_r, hn_s, hn_r, cu_s, cu_r, cd_s, cd_r,
    st_s, st_r, zs_s, zs_r, gs_s, gs_r, ct_s, ct_r, up_s, up_r, dn_s, dn_r,
):
    d = lax.axis_index("dp")
    me = lax.axis_index("cent")
    p, q = me // PLANE, me % PLANE
    x, y = q % 2, q // 2
    qx, qy, qd = q + 1 - 2 * x, q + 2 - 4 * y, 3 - q
    last = nz - 1
    blk, dim = cent_ref.shape
    half = blk // HALVES

    def at_plane(o):
        return {"cent": p * PLANE + o}

    def at_z(z):
        return {"cent": z * PLANE + q}

    def rows_at(o, b):
        return rbuf.at[pl.ds(pl.multiple_of((o * 2 + b) * BLK, BLK), BLK)]

    def remote(src, dst, s, r, to):
        return pltpu.make_async_remote_copy(
            src_ref=src, dst_ref=dst, send_sem=s, recv_sem=r, device_id=to, device_id_type=MESH
        )

    own_rows = pl.ds(pl.multiple_of(q * 2 * BLK, 2 * BLK), 2 * BLK)
    fetch = pltpu.make_async_copy(emb_ref, rbuf.at[own_rows], local_sem)
    fetch.start()

    barrier = pltpu.get_barrier_semaphore()
    for o in (qx, qy, qd):
        pl.semaphore_signal(barrier, inc=1, device_id=at_plane(o), device_id_type=MESH)
    for k in range(1, nz):
        pl.semaphore_signal(barrier, inc=1, device_id=at_z((p + k) % nz), device_id_type=MESH)
    for k in range(1, nd):
        pl.semaphore_signal(barrier, inc=1, device_id={"dp": (d + k) % nd}, device_id_type=MESH)

    cent = cent_ref[...]
    cbuf[p] = cent.astype(jnp.bfloat16)
    norm = 0.5 * jnp.sum(cent * cent, axis=1, keepdims=True)
    wide = jnp.broadcast_to(norm, (blk, 128))
    hncol[p] = wide
    hnrow[p] = wide.T[:8]
    maskbuf[pl.ds(q * 2, 2)] = mask_ref[...]
    fetch.wait()
    pl.semaphore_wait(barrier, 3 + (nz - 1) + (nd - 1))

    plane_peers = (qx, qy, qd)
    mine = maskbuf.at[pl.ds(q * 2, 2)]
    mask_out = [remote(mine, mine, mask_s.at[i], mask_r.at[i], at_plane(o)) for i, o in enumerate(plane_peers)]
    hn_out = [
        remote(hnrow.at[p], hnrow.at[p], hn_s.at[k - 1], hn_r.at[k - 1], at_z((p + k) % nz)) for k in range(1, nz)
    ]
    for c in mask_out + hn_out:
        c.start()

    def up_send(s):
        z = jnp.maximum(p - s, 0)
        return remote(cbuf.at[z], cbuf.at[z], cu_s.at[s], cu_r.at[s], at_z(jnp.minimum(p + 1, last)))

    def dn_send(s):
        z = jnp.minimum(p + s, last)
        return remote(cbuf.at[z], cbuf.at[z], cd_s.at[s], cd_r.at[s], at_z(jnp.maximum(p - 1, 0)))

    def up_wait(s):
        z = p - 1 - s
        remote(cbuf.at[z], cbuf.at[z], cu_s.at[s], cu_r.at[s], at_z(p - 1)).wait_recv()

    def dn_wait(s):
        z = p + 1 + s
        remote(cbuf.at[z], cbuf.at[z], cd_s.at[s], cd_r.at[s], at_z(p + 1)).wait_recv()

    def row_copy(i, o, b, to):
        return remote(rows_at(o, b), rows_at(o, b), row_s.at[i], row_r.at[i], at_plane(to))

    pl.when(p < last)(lambda: up_send(0).start())
    pl.when(p > 0)(lambda: dn_send(0).start())
    row_out = [
        row_copy(0, q, 0, qx),
        row_copy(1, q, 1, qy),
        row_copy(2, q, 1, qx),
        row_copy(3, q, 0, qy),
        row_copy(4, qx, 0, qy),
        row_copy(5, qy, 1, qx),
    ]
    for c in row_out[:4]:
        c.start()
    row_in = [
        row_copy(0, qx, 0, qx),
        row_copy(1, qy, 1, qy),
        row_copy(2, qx, 1, qx),
        row_copy(3, qy, 0, qy),
        row_copy(4, qd, 0, qy),
        row_copy(5, qd, 1, qx),
    ]

    for i, o in enumerate(plane_peers):
        there = maskbuf.at[pl.ds(o * 2, 2)]
        remote(there, there, mask_s.at[i], mask_r.at[i], at_plane(o)).wait_recv()
    for k in range(1, nz):
        z = (p + nz - k) % nz
        remote(hnrow.at[z], hnrow.at[z], hn_s.at[k - 1], hn_r.at[k - 1], at_z(z)).wait_recv()
        row = hnrow[z][:1]
        hncol[z] = jnp.broadcast_to(row, (128, blk)).T

    def pair(i, z):
        t, e = i // 2, i % 2
        mult = (t * (3 - t)) // 2
        late = mult * (t - 1)
        rel = t - late + mult * e
        b = e + late * (1 - 2 * e)
        rx, ry = rel % 2, rel // 2
        ox, oy = x + rx - 2 * x * rx, y + ry - 2 * y * ry
        ci = (oy * 2 + ox) * 2 + b
        start = pl.multiple_of(ci * BLK, BLK)
        dots = lax.dot_general(
            cbuf[z], rbuf[pl.ds(start, BLK), :], (((1,), (1,)), ((), ())), preferred_element_type=jnp.float32
        )
        bias = maskbuf[ci, pl.ds(z * PLANE + q, 1), :]
        bias = jnp.concatenate([bias] * (BLK // 128), axis=1)
        norm = jnp.concatenate([hncol[z]] * (BLK // 128), axis=1)
        logits = (dots - norm) * (1.0 / math.sqrt(dim)) + bias
        peak = jnp.max(logits, axis=0, keepdims=True)
        e_val = jnp.exp(logits - peak)
        pbuf[z, :, pl.ds(start, BLK)] = e_val
        mst[z, pl.ds(ci, 1), :] = peak
        sst[z, pl.ds(ci, 1), :] = jnp.sum(e_val, axis=0, keepdims=True)

    def pairs(row_lo, row_hi, z_lo, z_hi):
        count = (row_hi - row_lo) // 2

        def body(n, carry):
            i, z = row_lo + 2 * (n % count), z_lo + n // count
            pair(i, z)
            pair(i + 1, z)
            return carry

        lax.fori_loop(0, count * (z_hi - z_lo), body, 0)

    pairs(0, 2, p, p + 1)
    for s in range(last):
        @pl.when(p - 1 - s >= 0)
        def _(s=s):
            up_wait(s)
            if s + 1 < last:
                pl.when(p < last)(lambda: up_send(s + 1).start())

        @pl.when(p + 1 + s <= last)
        def _(s=s):
            dn_wait(s)
            if s + 1 < last:
                pl.when(p > 0)(lambda: dn_send(s + 1).start())

        row_in[2 * s].wait_recv()
        row_in[2 * s + 1].wait_recv()
        if s == 0:
            row_out[4].start()
            row_out[5].start()
        have = 2 * s + 2

        @pl.when(p - 1 - s >= 0)
        def _(s=s, have=have):
            pairs(0, have, p - 1 - s, p - s)

        @pl.when(p + 1 + s <= last)
        def _(s=s, have=have):
            pairs(0, have, p + 1 + s, p + 2 + s)

        pairs(have, have + 2, jnp.maximum(p - s - 1, 0), jnp.minimum(p + s + 1, last) + 1)

    peak, total = mst[0], sst[0]
    for z in range(1, nz):
        peak = jnp.maximum(peak, mst[z])
    total = sum(sst[z] * jnp.exp(mst[z] - peak) for z in range(nz))
    stat[q, 0] = peak
    stat[q, 1] = total
    st_out = [
        remote(stat.at[q], stat.at[q], st_s.at[i], st_r.at[i], at_plane(o)) for i, o in enumerate(plane_peers)
    ]
    for c in st_out:
        c.start()
    for i, o in enumerate(plane_peers):
        remote(stat.at[o], stat.at[o], st_s.at[i], st_r.at[i], at_plane(o)).wait_recv()
    peak = stat[0, 0]
    for o in range(1, PLANE):
        peak = jnp.maximum(peak, stat[o, 0])
    total = sum(stat[o, 1] * jnp.exp(stat[o, 0] - peak) for o in range(PLANE))
    log_norm = peak + jnp.log(total)
    place = lax.broadcasted_iota(jnp.int32, log_norm.shape, 0)
    for r in range(2):
        log_ref[r : r + 1, :] = jnp.sum(jnp.where(place == q * 2 + r, log_norm, 0.0), axis=0, keepdims=True)
    for z in range(nz):
        fbuf[z] = jnp.exp(mst[z] - log_norm)
    zsum[p] = jnp.broadcast_to(jnp.sum(jnp.sum(log_norm, axis=1, keepdims=True), axis=0, keepdims=True), (8, 128))
    zs_out = [
        remote(zsum.at[p], zsum.at[p], zs_s.at[k - 1], zs_r.at[k - 1], at_z((p + k) % nz)) for k in range(1, nz)
    ]
    for c in zs_out:
        c.start()

    def partial(t):
        cacc[...] = jnp.zeros_like(cacc)

        def weigh(ci, carry):
            cols = pl.ds(pl.multiple_of(ci * BLK, BLK), BLK)
            w = pbuf[t, :, cols] * fbuf[t, pl.ds(ci, 1), :]
            wbuf[:, cols] = w.astype(jnp.bfloat16)
            acc = cacc[...]
            for j in range(BLK // 128):
                acc = acc + w[:, j * 128 : (j + 1) * 128]
            cacc[...] = acc
            return carry

        lax.fori_loop(0, 2 * PLANE, weigh, 0)
        col = jnp.broadcast_to(jnp.sum(cacc[...], axis=1, keepdims=True), (blk, 128))
        cnt[t] = col.T[:8]

        def tile(n, carry):
            cols = pl.ds(pl.multiple_of(n * BLK, BLK), BLK)
            part[t, :, cols] = jnp.dot(wbuf[...], rbuf[:, cols], preferred_element_type=jnp.float32)
            return carry

        lax.fori_loop(0, dim // BLK, tile, 0)

    def up_copy(t, h):
        part_of = (t, pl.ds(h * half, half))
        return remote(
            tx.at[part_of], up_rx.at[part_of], up_s.at[t, h], up_r.at[t, h], at_z(jnp.minimum(p + 1, last))
        )

    def dn_copy(t, h):
        part_of = (t, pl.ds(h * half, half))
        return remote(tx.at[part_of], dn_rx.at[part_of], dn_s.at[t, h], dn_r.at[t, h], at_z(jnp.maximum(p - 1, 0)))

    up_order = [(last - s, h) for s in range(last) for h in range(HALVES)]
    dn_order = [(s, h) for s in range(last) for h in range(HALVES)]

    for s in range(last):
        up_t, dn_t = last - s, s

        @pl.when(p < up_t)
        def _(t=up_t):
            partial(t)

            @pl.when(p == 0)
            def _():
                tx[t] = part[t].astype(jnp.bfloat16)
                if t == last:
                    for n in range(2):
                        up_copy(*up_order[n]).start()

        @pl.when(p > dn_t)
        def _(t=dn_t):
            partial(t)

            @pl.when(p == last)
            def _():
                tx[t] = part[t].astype(jnp.bfloat16)
                if t == 0:
                    for n in range(2):
                        dn_copy(*dn_order[n]).start()

    partial(p)

    cnt_rx[p] = cnt[p]
    ct_out = [
        remote(cnt.at[(p + k) % nz], cnt_rx.at[p], ct_s.at[k - 1], ct_r.at[k - 1], at_z((p + k) % nz))
        for k in range(1, nz)
    ]
    for c in ct_out:
        c.start()

    for k in range(1, nz):
        z = (p + nz - k) % nz
        remote(zsum.at[z], zsum.at[z], zs_s.at[k - 1], zs_r.at[k - 1], at_z(z)).wait_recv()
    gsum[d] = sum(zsum[z] for z in range(nz))
    gs_out = [
        remote(gsum.at[d], gsum.at[d], gs_s.at[k - 1], gs_r.at[k - 1], {"dp": (d + k) % nd}) for k in range(1, nd)
    ]
    for c in gs_out:
        c.start()

    for n in range(len(up_order)):
        up_t, dn_t = up_order[n][0], dn_order[n][0]

        @pl.when((p > 0) & (p < up_t))
        def _(t=up_t, h=up_order[n][1]):
            up_copy(t, h).wait_recv()
            rows = pl.ds(h * half, half)
            tx[t, rows] = (part[t, rows] + up_rx[t, rows].astype(jnp.float32)).astype(jnp.bfloat16)
            up_copy(t, h).start()

        @pl.when((p < last) & (p > dn_t))
        def _(t=dn_t, h=dn_order[n][1]):
            dn_copy(t, h).wait_recv()
            rows = pl.ds(h * half, half)
            tx[t, rows] = (part[t, rows] + dn_rx[t, rows].astype(jnp.float32)).astype(jnp.bfloat16)
            dn_copy(t, h).start()

        if n >= 2:
            @pl.when(p == 0)
            def _(n=n):
                up_copy(*up_order[n - 2]).wait_send()
                up_copy(*up_order[n]).start()

            @pl.when(p == last)
            def _(n=n):
                dn_copy(*dn_order[n - 2]).wait_send()
                dn_copy(*dn_order[n]).start()

    for k in range(1, nz):
        z = (p + nz - k) % nz
        remote(cnt.at[z], cnt_rx.at[z], ct_s.at[k - 1], ct_r.at[k - 1], at_z(z)).wait_recv()
    counts = sum(cnt_rx[z] for z in range(nz))
    scale = 1.0 / (jnp.broadcast_to(counts[:1], (128, blk)).T[:, :1] + 1.0)
    for k in range(1, nd):
        o = (d + nd - k) % nd
        remote(gsum.at[o], gsum.at[o], gs_s.at[k - 1], gs_r.at[k - 1], {"dp": o}).wait_recv()
    obj_ref[...] = sum(gsum[o] for o in range(nd)) / row_total

    new_ref[...] = cent_ref[...] + part[p]
    for h in range(HALVES):
        rows = pl.ds(h * half, half)

        @pl.when(p > 0)
        def _(h=h, rows=rows):
            up_copy(p, h).wait_recv()
            new_ref[rows, :] += up_rx[p, rows].astype(jnp.float32)

        @pl.when(p < last)
        def _(h=h, rows=rows):
            dn_copy(p, h).wait_recv()
            new_ref[rows, :] += dn_rx[p, rows].astype(jnp.float32)

    new_ref[...] = new_ref[...] * scale

    for c in mask_out + hn_out + row_out + st_out + zs_out + ct_out + gs_out:
        c.wait_send()
    for s in range(last):
        pl.when((p < last) & (p - s >= 0))(lambda s=s: up_send(s).wait_send())
        pl.when((p > 0) & (p + s <= last))(lambda s=s: dn_send(s).wait_send())
    tail = len(up_order) - 2
    for n in range(len(up_order)):
        up_t, dn_t = up_order[n][0], dn_order[n][0]
        pl.when((p < up_t) & ((p > 0) | (n >= tail)))(lambda n=n: up_copy(*up_order[n]).wait_send())
        pl.when((p > dn_t) & ((p < last) | (n >= tail)))(lambda n=n: dn_copy(*dn_order[n]).wait_send())


def per_device(embeddings, centroids, candidates):
    nd, nc = lax.axis_size("dp"), lax.axis_size("cent")
    nz = nc // PLANE
    dim = embeddings.shape[1]
    rows = embeddings.shape[0]
    rb = candidates.shape[0]
    named = jnp.any(candidates[:, :, None] == jnp.arange(nc, dtype=jnp.int32), axis=1)
    mask = jnp.broadcast_to(jnp.where(named, 0.0, FLOOR).astype(jnp.float32)[:, :, None], (rb, nc, 128))
    f32, bf16 = jnp.float32, jnp.bfloat16
    nrb = rb * PLANE
    dma = pltpu.SemaphoreType.DMA
    vmem = pl.BlockSpec(memory_space=pltpu.VMEM)
    new, logs, obj = pl.pallas_call(
        functools.partial(kernel, nd, nz, float(rows * nd * nc)),
        out_shape=(
            jax.ShapeDtypeStruct((BLK, dim), f32),
            jax.ShapeDtypeStruct((rb, BLK), f32),
            jax.ShapeDtypeStruct((8, 128), f32),
        ),
        in_specs=[pl.BlockSpec(memory_space=pl.ANY), vmem, vmem],
        out_specs=(vmem, vmem, vmem),
        scratch_shapes=[
            pltpu.VMEM((nrb * BLK, dim), bf16),
            pltpu.VMEM((nz, BLK, dim), bf16),
            pltpu.VMEM((nz, 8, BLK), f32),
            pltpu.VMEM((nz, BLK, 128), f32),
            pltpu.VMEM((nrb, nc, 128), f32),
            pltpu.VMEM((nz, BLK, nrb * BLK), f32),
            pltpu.VMEM((nz, nrb, BLK), f32),
            pltpu.VMEM((nz, nrb, BLK), f32),
            pltpu.VMEM((PLANE, 2, nrb, BLK), f32),
            pltpu.VMEM((nz, nrb, BLK), f32),
            pltpu.VMEM((BLK, nrb * BLK), bf16),
            pltpu.VMEM((nz, BLK, dim), f32),
            pltpu.VMEM((nz, BLK, dim), bf16),
            pltpu.VMEM((nz, BLK, dim), bf16),
            pltpu.VMEM((nz, BLK, dim), bf16),
            pltpu.VMEM((BLK, 128), f32),
            pltpu.VMEM((nz, 8, BLK), f32),
            pltpu.VMEM((nz, 8, BLK), f32),
            pltpu.VMEM((nz, 8, 128), f32),
            pltpu.VMEM((nd, 8, 128), f32),
            dma(()),
            dma((6,)), dma((6,)),
            dma((3,)), dma((3,)),
            dma((nz - 1,)), dma((nz - 1,)),
            dma((nz - 1,)), dma((nz - 1,)),
            dma((nz - 1,)), dma((nz - 1,)),
            dma((3,)), dma((3,)),
            dma((nz - 1,)), dma((nz - 1,)),
            dma((max(nd - 1, 1),)), dma((max(nd - 1, 1),)),
            dma((nz - 1,)), dma((nz - 1,)),
            dma((nz, HALVES)), dma((nz, HALVES)),
            dma((nz, HALVES)), dma((nz, HALVES)),
        ],
        compiler_params=pltpu.CompilerParams(
            collective_id=0, has_side_effects=True, vmem_limit_bytes=48 * 1024 * 1024
        ),
    )(embeddings, centroids, mask)
    return new, logs.reshape(rows), obj[0, 0]


def solution(mesh):
    in_specs = (P(("dp", "cent"), None), P(("dp", "cent"), None), P(("dp", "cent"), None))
    out_specs = (P(("dp", "cent"), None), P(("dp", "cent")), P())
    return jax.shard_map(
        per_device, mesh=mesh, in_specs=in_specs, out_specs=out_specs, check_vma=False
    )
```
